512 devices in a mesh: expert: 2 (over y_hi), cfg: 2 (over core), rep: 16 (over x, y_lo), sp: 8 (over z).
Axes of the slice: x: 4, y: 8 (y_hi: 2, y_lo: 4; y = y_hi * 4 + y_lo), z: 8, core: 2. Of those that a mesh axis runs over, the one named last changes fastest.
Arguments:
- queries: bfloat16 [2, 2, 10240, 3072], P('expert', None, ('rep', 'cfg', 'sp')), parts along dimension 2, may hold values from -600 to 600
- keys: bfloat16 [2, 2, 10240, 3072], P('expert', None, ('rep', 'cfg', 'sp')), parts along dimension 2, may hold values from -600 to 600
- values: bfloat16 [2, 2, 10240, 3072], P('expert', None, ('rep', 'cfg', 'sp')), parts along dimension 2, may hold values from -600 to 600
- cross_queries: bfloat16 [2, 2, 10240, 3072], P('expert', None, ('rep', 'cfg', 'sp')), parts along dimension 2, may hold values from -600 to 600
- q_gain: float32 [2, 3072], P('expert'), may hold values from 0.1 to 1.9
- k_gain: float32 [2, 3072], P('expert'), may hold values from 0.1 to 1.9
- cross_gain: float32 [2, 3072], P('expert'), may hold values from 0.1 to 1.9
- text_keys: bfloat16 [2, 2, 4096, 3072], P('expert', 'cfg', 'rep', 'sp'), parts along dimension 2, may hold values from -48 to 48
- text_values: bfloat16 [2, 2, 4096, 3072], P('expert', 'cfg', 'rep', 'sp'), parts along dimension 2, may hold values from -5 to 5
- text_lengths: int32 [2, 2, 16], P('expert', 'cfg', 'rep'), parts along dimension 2, may hold values from 1 to 256, as said below
- step_index: int32 [2, 16], P('expert', 'rep'), parts along dimension 1, may hold values from 0 to 39, as said below
- latent: float32 [2, 10240, 64], P('expert', ('rep', 'cfg', 'sp')), parts along dimension 1, may hold values from -5 to 5
- head_weight: bfloat16 [2, 3072, 64], P('expert', 'sp'), may hold values from -0.109375 to 0.109375
Outputs:
- clean_estimate: float32 [2, 10240, 64], P('expert', ('rep', 'cfg', 'sp')), parts along dimension 1
- handed_latent: bfloat16 [2, 10240, 64], P('expert', ('rep', 'cfg', 'sp')), parts along dimension 1
- handed_keys: bfloat16 [2, 2, 4096, 3072], P('expert', 'cfg', 'rep', 'sp'), parts along dimension 2
- handed_values: bfloat16 [2, 2, 4096, 3072], P('expert', 'cfg', 'rep', 'sp'), parts along dimension 2
The draws below stay inside these ranges and needn't reach their ends.
There are 16 independent parts, one for each index of `rep`. The reference program is written for one: setup_inputs(seed, part) draws one part's arguments, and reference() takes and returns one part's arrays. A program takes and returns all parts, laid end to end along the dimension named above; an argument that names none is the same for every part. Nothing has to cross between parts.
Inputs may be any that keep to these rules, and one draw needn't show every extreme that they name: `text_lengths`: one entry equals 256. `step_index`: entry 0, the high-noise batch, is below 26; entry 1 is 26 or more.
All inputs are finite; a program needn't handle non-finite values.
Results may differ from the reference program's by a relative error of at most 0.0068.
Values may be sent and summed in bfloat16 or wider, within the bound.
A program may use at most 64 MiB of HBM per device.

```python
import math
import jax
import jax.numpy as jnp
from jax import lax

HEADS = 24
HEAD = 128
D = 3072
LC = 64
TEXT = 256
STEPS = 40
SWITCH = 26
TOKENS = 640


def spread_rows(key, base, top_scale):
    row_key, col_key = jax.random.split(key)
    row_scale = jnp.exp(jax.random.uniform(row_key, base.shape[:-1] + (1,), jnp.float32, 0.0, math.log(top_scale)))
    col_scale = jnp.exp(jax.random.uniform(col_key, base.shape[:-2] + (1, base.shape[-1]), jnp.float32, 0.0, math.log(top_scale)))
    return base * row_scale * col_scale


def drawn_base(base_key, shape):
    return jnp.clip(jax.random.normal(base_key, shape, jnp.float32), -5.0, 5.0)


def draw_queries(key, part):
    key = jax.random.fold_in(key, 11)
    base_key = jax.random.fold_in(key, 0)
    spread_key = jax.random.fold_in(key, 2)
    shape = (2, 2, TOKENS, D)
    field = spread_rows(spread_key, drawn_base(base_key, shape), 10.0)
    return field.astype(jnp.bfloat16)


def draw_keys(key, part):
    key = jax.random.fold_in(key, 12)
    base_key = jax.random.fold_in(key, 0)
    spread_key = jax.random.fold_in(key, 2)
    shape = (2, 2, TOKENS, D)
    field = spread_rows(spread_key, drawn_base(base_key, shape), 10.0)
    return field.astype(jnp.bfloat16)


def draw_values(key, part):
    key = jax.random.fold_in(key, 13)
    base_key = jax.random.fold_in(key, 0)
    spread_key = jax.random.fold_in(key, 2)
    shape = (2, 2, TOKENS, D)
    field = spread_rows(spread_key, drawn_base(base_key, shape), 10.0)
    return field.astype(jnp.bfloat16)


def draw_cross_queries(key, part):
    key = jax.random.fold_in(key, 14)
    base_key = jax.random.fold_in(key, 0)
    spread_key = jax.random.fold_in(key, 2)
    shape = (2, 2, TOKENS, D)
    field = spread_rows(spread_key, drawn_base(base_key, shape), 10.0)
    return field.astype(jnp.bfloat16)


def draw_text_keys(key, part):
    key = jax.random.fold_in(key, 15)
    base_key = jax.random.fold_in(key, 0)
    shape = (2, 2, TEXT, D)
    field = drawn_base(base_key, shape)
    return field.astype(jnp.bfloat16)


def draw_text_lengths(key, part):
    key = jax.random.fold_in(key, 16)
    length_key, pick_key = jax.random.split(key)
    drawn = jax.random.randint(length_key, (4,), 1, TEXT + 1)
    picked = jax.random.randint(pick_key, (), 0, 4)
    drawn = jnp.where(jnp.arange(4) == picked, TEXT, drawn)
    return drawn.reshape(2, 2, 1).astype(jnp.int32)


def draw_step_index(key, part):
    key = jax.random.fold_in(key, 17)
    high_key, low_key = jax.random.split(key)
    high_step = jax.random.randint(high_key, (1,), 0, SWITCH)
    low_step = jax.random.randint(low_key, (1,), SWITCH, STEPS)
    return jnp.stack([high_step, low_step]).astype(jnp.int32)


def level_of(key, dims, pieces, low, largest):
    def one(position, blocks):
        heights = jax.random.uniform(jax.random.fold_in(jax.random.fold_in(key, 6), position), (blocks,), jnp.float32, low / len(pieces), largest / len(pieces))
        return jnp.repeat(jnp.exp(heights), dims[position] // blocks).reshape((-1,) + (1,) * (len(dims) - position - 1))

    gain = one(*pieces[0])
    for cut in pieces[1:]:
        gain = gain * one(*cut)
    return gain


def bell_draw(stream_key, dims, deviation, bound, shards=(), kind=jnp.bfloat16):
    values = jax.random.normal(stream_key, dims, jnp.float32) * deviation
    if len(shards) > 0:
        values = level_of(stream_key, dims, shards, -0.22, 0.18) * values
    return jnp.clip(values, min=-bound, max=bound).astype(kind)


def setup_inputs(seed: int = 0, part: int = 0) -> dict:
    streams_of = jax.random.split(jax.random.key(seed), 14)
    own_keys = jax.random.split(jax.random.fold_in(streams_of[13], part), 14)
    queries = draw_queries(jax.random.fold_in(jax.random.fold_in(streams_of[13], part), 71), part)
    keys = draw_keys(jax.random.fold_in(jax.random.fold_in(streams_of[13], part), 71), part)
    values = draw_values(jax.random.fold_in(jax.random.fold_in(streams_of[13], part), 71), part)
    cross_queries = draw_cross_queries(jax.random.fold_in(jax.random.fold_in(streams_of[13], part), 71), part)
    q_gain = jnp.clip(1.0 + 0.18 * jax.random.normal(streams_of[4], (2, D), jnp.float32), 0.1, 1.9)
    k_gain = jnp.clip(1.0 + 0.18 * jax.random.normal(streams_of[5], (2, D), jnp.float32), 0.1, 1.9)
    cross_gain = jnp.clip(1.0 + 0.18 * jax.random.normal(streams_of[6], (2, D), jnp.float32), 0.1, 1.9)
    text_keys = draw_text_keys(jax.random.fold_in(jax.random.fold_in(streams_of[13], part), 71), part)
    text_values = bell_draw(own_keys[8], (2, 2, TEXT, D), 1.0, 5.0, ((0, 2), (1, 2), (3, 8)))
    text_lengths = draw_text_lengths(jax.random.fold_in(jax.random.fold_in(streams_of[13], part), 71), part)
    step_index = draw_step_index(jax.random.fold_in(jax.random.fold_in(streams_of[13], part), 71), part)
    latent = bell_draw(own_keys[11], (2, TOKENS, LC), 1.0, 5.0, ((0, 2), (1, 16)), jnp.float32)
    head_weight = bell_draw(streams_of[12], (2, D, LC), D ** -0.5, 0.109375, ((0, 2), (1, 8)))
    return {"queries": queries, "keys": keys, "values": values, "cross_queries": cross_queries, "q_gain": q_gain, "k_gain": k_gain, "cross_gain": cross_gain, "text_keys": text_keys, "text_values": text_values, "text_lengths": text_lengths, "step_index": step_index, "latent": latent, "head_weight": head_weight}


TIME_SHIFT = 12.0
HIGH_GUIDE = 4.0
LOW_GUIDE = 3.0
NORM_EPS = 1e-06

def sigma_at(index):
    frac = 1.0 - index.astype(jnp.float32) / STEPS
    return TIME_SHIFT * frac / (1.0 + (TIME_SHIFT - 1.0) * frac)

def rms_norm(features, gain_row):
    return features * lax.rsqrt(lax.optimization_barrier(jnp.mean(features * features, axis=-1, keepdims=True)) + NORM_EPS) * gain_row

def rotary(features, positions):
    column = jnp.arange(features.shape[-1])
    pair_index = (column % HEAD // 2).astype(jnp.float32)
    freq = jnp.exp(-(2.0 * pair_index / HEAD) * math.log(10000.0))
    angle = positions[:, None] * freq[None, :]
    partner = jnp.where(column % 2 == 0, -jnp.roll(features, -1, axis=-1), jnp.roll(features, 1, axis=-1))
    return features * jnp.cos(angle) + partner * jnp.sin(angle)

def attention(query_heads, key_heads, value_heads, key_mask):
    scores = jnp.einsum('qhd,khd->hqk', query_heads.astype(jnp.float32), key_heads.astype(jnp.float32)) / math.sqrt(HEAD)
    scores = jnp.where(key_mask[None, None, :], scores, -jnp.inf)
    row_max = lax.optimization_barrier(jnp.max(scores, axis=-1, keepdims=True))
    exponent = jnp.exp(scores - row_max)
    weights = (exponent / lax.optimization_barrier(jnp.sum(exponent, axis=-1, keepdims=True))).astype(jnp.bfloat16)
    return jnp.einsum('hqk,khd->qhd', weights.astype(jnp.float32), value_heads.astype(jnp.float32))

def reference(queries, keys, values, cross_queries, q_gain, k_gain, cross_gain, text_keys, text_values, text_lengths, step_index, latent, head_weight):
    positions = jnp.arange(TOKENS).astype(jnp.float32)
    text_rows = jnp.arange(TEXT)
    all_keys = jnp.ones((TOKENS,), dtype=bool)
    head_shape = (TOKENS, HEADS, HEAD)
    text_shape = (TEXT, HEADS, HEAD)
    cleans = []
    stepped_list = []
    kept_keys = []
    kept_values = []
    for expert in range(2):
        velocities = []
        for branch in range(2):
            query_rot = rotary(rms_norm(queries[expert, branch].astype(jnp.float32), q_gain[expert]), positions).astype(jnp.bfloat16)
            key_rot = rotary(rms_norm(keys[expert, branch].astype(jnp.float32), k_gain[expert]), positions).astype(jnp.bfloat16)
            cross_norm = rms_norm(cross_queries[expert, branch].astype(jnp.float32), cross_gain[expert]).astype(jnp.bfloat16)
            self_out = attention(query_rot.reshape(head_shape), key_rot.reshape(head_shape), values[expert, branch].reshape(head_shape), all_keys)
            text_mask = text_rows < text_lengths[expert, branch, 0]
            cross_out = attention(cross_norm.reshape(head_shape), text_keys[expert, branch].reshape(text_shape), text_values[expert, branch].reshape(text_shape), text_mask)
            hidden = lax.optimization_barrier((self_out + cross_out).reshape(TOKENS, D).astype(jnp.bfloat16))
            hidden_f = hidden.astype(jnp.float32)
            centred = hidden_f - lax.optimization_barrier(jnp.mean(hidden_f, axis=-1, keepdims=True))
            normed = centred * lax.rsqrt(lax.optimization_barrier(jnp.mean(centred * centred, axis=-1, keepdims=True)) + NORM_EPS)
            velocities.append(jnp.dot(normed, head_weight[expert].astype(jnp.float32), precision=lax.Precision.HIGHEST))
        guide_scale = HIGH_GUIDE if expert == 0 else LOW_GUIDE
        guided = velocities[1] + guide_scale * (velocities[0] - velocities[1])
        sigma_now = sigma_at(step_index[expert, 0])
        sigma_next = sigma_at(step_index[expert, 0] + 1)
        cleans.append(latent[expert] - sigma_now * guided)
        stepped_list.append((latent[expert] + (sigma_next - sigma_now) * guided).astype(jnp.bfloat16))
        keep_rows = (text_rows[None, :] < text_lengths[expert, :, 0][:, None])[:, :, None]
        kept_keys.append(jnp.where(keep_rows, text_keys[expert], jnp.zeros_like(text_keys[expert])))
        kept_values.append(jnp.where(keep_rows, text_values[expert], jnp.zeros_like(text_values[expert])))
    clean_estimate = jnp.stack(cleans)
    handed_latent = jnp.stack([stepped_list[1], stepped_list[0]])
    handed_keys = jnp.stack([kept_keys[1], kept_keys[0]])
    handed_values = jnp.stack([kept_values[1], kept_values[0]])
    return (clean_estimate, handed_latent, handed_keys, handed_values)
```

```python
import math

import jax
import jax.numpy as jnp
from jax import lax
from jax.experimental import pallas as pl
from jax.experimental.pallas import tpu as pltpu
from jax.sharding import PartitionSpec as P

HEAD = 128
STEPS = 40
TIME_SHIFT = 12.0
HIGH_GUIDE = 4.0
LOW_GUIDE = 3.0
NORM_EPS = 1e-06

MESH = pl.DeviceIdType.MESH
BF16 = jnp.bfloat16
F32 = jnp.float32
RING = (4, 3, 5, 2, 6, 1, 7)
V, K, Q, C, R = range(5)


def sigma_at(index):
    frac = 1.0 - index / STEPS
    return TIME_SHIFT * frac / (1.0 + (TIME_SHIFT - 1.0) * frac)


def contract_last(a, b):
    return lax.dot_general(a, b, (((1,), (1,)), ((), ())), preferred_element_type=F32)


def body(n, rows, heads, *refs):
    (
        q_hbm, k_hbm, v_hbm, c_hbm, qg_hbm, kg_hbm, cg_hbm, tk_hbm, tv_hbm, len_hbm, step_hbm, lat_hbm, w_hbm,
        clean_out, hlat_out, hk_out, hv_out,
        q_in, k_in, c_in, qg, kg, cg, tk, tv, length, step, lat, w_in,
        q_src, k_src, c_src, v_dst, k_dst, q_dst, c_dst,
        kr, qr, cr, va, tva, self_o, hid, cos_t, sin_t,
        tk_m, tv_m, wcat, col_src, col_dst, p_src, p_dst, clean_v, step_v,
        load_sem, send_sem, recv_sem, col_send, col_recv, x_send, x_recv, out_sem,
    ) = refs
    local = heads // n
    width = local * HEAD
    e = lax.axis_index("expert")
    c = lax.axis_index("cfg")
    z = lax.axis_index("sp")

    def chip(d):
        return lax.rem(z + d, n)

    def core(x):
        return lax.rem(c + x, 2)

    remote = [(d, x) for d in RING for x in (0, 1)] + [(0, 1)]

    barrier = pltpu.get_barrier_semaphore()
    for d, x in remote:
        pl.semaphore_signal(barrier, 1, device_id={"cfg": core(x), "sp": chip(d)}, device_id_type=MESH)
    pl.semaphore_signal(barrier, 1, device_id={"expert": 1 - e}, device_id_type=MESH)

    loads = []
    for i, (src, dst) in enumerate(
        (
            (k_hbm.at[0], k_in), (kg_hbm, kg), (q_hbm.at[0], q_in), (qg_hbm, qg), (c_hbm.at[0], c_in), (cg_hbm, cg),
            (tk_hbm.at[0, 0], tk), (tv_hbm.at[0, 0], tv), (len_hbm, length), (step_hbm, step), (lat_hbm.at[0], lat),
            (w_hbm.at[0], w_in),
        )
    ):
        copy = pltpu.make_async_copy(src, dst, load_sem.at[i])
        copy.start()
        loads.append(copy)

    sends = []

    def move(a, d, x, src, dst):
        if (d, x) == (0, 0):
            copy = pltpu.make_async_copy(src, dst, recv_sem.at[a, 0, 0])
            copy.start()
            return
        copy = pltpu.make_async_remote_copy(
            src, dst, send_sem.at[a, d, x], recv_sem.at[a, d, x],
            device_id={"cfg": core(x), "sp": chip(d)}, device_id_type=MESH,
        )
        copy.start()
        sends.append(copy)

    def arrived(a, d, x, ref):
        pltpu.make_async_copy(ref, ref, recv_sem.at[a, d, x]).wait()

    def v_move(d, x):
        cols = pl.ds(pl.multiple_of(chip(d) * width, HEAD), width)
        move(V, d, x, v_hbm.at[0, core(x), :, cols], v_dst.at[z, c])

    v_move(0, 0)
    pl.semaphore_wait(barrier, len(remote) + 1)
    for d, x in remote:
        v_move(d, x)

    lane = lax.broadcasted_iota(jnp.int32, (rows, HEAD), 1)
    even = lax.rem(lane, 2) == 0
    row = lax.broadcasted_iota(jnp.int32, (rows, HEAD), 0)
    position = ((c * n + z) * rows + row).astype(F32)
    pair = (lane // 2).astype(F32)
    angle = position * jnp.exp(-(2.0 * pair / HEAD) * math.log(10000.0))
    cos_t[...] = jnp.cos(angle)
    sin = jnp.sin(angle)
    sin_t[...] = jnp.where(even, -sin, sin)

    def prepare(x_ref, g_ref, o_ref, rope):
        for b in range(2):

            def square(i, total):
                for j in range(local):
                    cols = pl.ds(pl.multiple_of(i * width + j * HEAD, HEAD), HEAD)
                    x = x_ref[b, :, cols].astype(F32)
                    total = total + x * x
                return total

            total = lax.fori_loop(0, n, square, jnp.zeros((rows, HEAD), F32))
            scale = lax.rsqrt(jnp.sum(total, axis=-1, keepdims=True) / (heads * HEAD) + NORM_EPS)

            def one(i, carry):
                for j in range(local):
                    cols = pl.ds(pl.multiple_of(i * width + j * HEAD, HEAD), HEAD)
                    x = x_ref[b, :, cols].astype(F32) * scale * g_ref[:, cols]
                    if rope:
                        partner = jnp.where(even, pltpu.roll(x, HEAD - 1, 1), pltpu.roll(x, 1, 1))
                        x = x * cos_t[...] + partner * sin_t[...]
                    o_ref[b, i * local + j] = x.astype(BF16)
                return carry

            lax.fori_loop(0, n, one, 0)

    def spread(a, src, dst):
        for d, x in [*remote, (0, 0)]:
            move(a, d, x, src.at[core(x), pl.ds(chip(d) * local, local)], dst.at[:, z, c])

    loads[0].wait()
    loads[1].wait()
    prepare(k_in, kg, k_src, True)
    spread(K, k_src, k_dst)
    loads[2].wait()
    loads[3].wait()
    prepare(q_in, qg, q_src, True)
    spread(Q, q_src, q_dst)
    loads[4].wait()
    loads[5].wait()
    prepare(c_in, cg, c_src, False)
    spread(C, c_src, c_dst)

    for i in range(6, 12):
        loads[i].wait()
    count = length[0, 0, 0]
    text = tk.shape[0]
    keep = lax.broadcasted_iota(jnp.int32, (text, width), 0) < count
    tk_m[...] = jnp.where(keep, tk[...].astype(F32), 0.0).astype(BF16)
    tv_m[...] = jnp.where(keep, tv[...].astype(F32), 0.0).astype(BF16)
    handed = []
    for i, (src, dst) in enumerate(((tk_m, hk_out.at[0, 0]), (tv_m, hv_out.at[0, 0]))):
        copy = pltpu.make_async_remote_copy(
            src, dst, x_send.at[i], x_recv.at[i], device_id={"expert": 1 - e}, device_id_type=MESH
        )
        copy.start()
        handed.append(copy)

    w = w_in[...].astype(F32)
    wcat[:, 0:HEAD] = jnp.concatenate([w, w], axis=1).astype(BF16)
    wcat[:, HEAD : 2 * HEAD] = jnp.ones((width, HEAD), BF16)
    col_src[...] = jnp.dot(jnp.ones((8, width), BF16), wcat[:, 0:HEAD], preferred_element_type=F32)
    col_dst[z] = col_src[...]
    for d in RING:
        copy = pltpu.make_async_remote_copy(
            col_src, col_dst.at[z], col_send.at[d], col_recv.at[d], device_id={"sp": chip(d)}, device_id_type=MESH
        )
        copy.start()
        sends.append(copy)

    for h in range(local):
        tva[h, :, 0:HEAD] = tv[:, h * HEAD : (h + 1) * HEAD]
        tva[h, :, HEAD : 2 * HEAD] = jnp.ones((text, HEAD), BF16)
        va[h, :, HEAD : 2 * HEAD] = jnp.ones((va.shape[1], HEAD), BF16)

    everyone = [(d, x) for d in (0, *RING) for x in (0, 1)]
    pair_rows = 2 * rows

    for d, x in everyone:
        arrived(V, d, x, v_dst.at[chip(n - d), core(x)])
    for s in range(n):
        for h in range(local):
            block = v_dst[s, :, :, h * HEAD : (h + 1) * HEAD].astype(F32)
            va[h, s * pair_rows : (s + 1) * pair_rows, 0:HEAD] = block.reshape(pair_rows, HEAD).astype(BF16)

    def gather(a, dst, out):
        for d, x in everyone:
            arrived(a, d, x, dst.at[:, chip(n - d), core(x)])
        for h in range(local):
            for s in range(n):
                block = dst[h, s].astype(F32)
                out[h, s * pair_rows : (s + 1) * pair_rows, :] = block.reshape(pair_rows, HEAD).astype(BF16)

    gather(K, k_dst, kr)
    gather(Q, q_dst, qr)
    factor = math.log2(math.e) / math.sqrt(HEAD)
    step_rows = 2 * pair_rows
    blocks = n // 2
    for h in range(local):
        for r in range(blocks):
            part = slice(r * step_rows, (r + 1) * step_rows)
            s = contract_last(qr[h, part, :], kr[h])
            p = jnp.exp2((s - jnp.max(s, axis=-1, keepdims=True)) * factor).astype(BF16)
            o = jnp.dot(p, va[h], preferred_element_type=F32)
            self_o[h, part, :] = o[:, 0:HEAD] / o[:, HEAD : 2 * HEAD]

    gather(C, c_dst, cr)
    used = lax.broadcasted_iota(jnp.int32, (step_rows, text), 1) < count
    out_lane = lax.broadcasted_iota(jnp.int32, (step_rows, HEAD), 1)
    half = HEAD // 2
    order = (4, 3, 5, 2, 6, 1, 7, 0)
    for r in range(blocks):
        pair_of = order[2 * r : 2 * r + 2]
        starts = [pl.multiple_of(chip(d) * pair_rows, pair_rows) for d in pair_of]

        def take(ref, h):
            return jnp.concatenate([ref[h, pl.ds(start, pair_rows), :] for start in starts], axis=0)

        for h in range(local):
            s = contract_last(take(cr, h), tk[:, h * HEAD : (h + 1) * HEAD])
            s = jnp.where(used, s, -jnp.inf)
            p = jnp.exp2((s - jnp.max(s, axis=-1, keepdims=True)) * factor).astype(BF16)
            o = jnp.dot(p, tva[h], preferred_element_type=F32)
            hid[:, h * HEAD : (h + 1) * HEAD] = (take(self_o, h) + o[:, 0:HEAD] / o[:, HEAD : 2 * HEAD]).astype(BF16)
        both = jnp.dot(hid[...], wcat[...], preferred_element_type=F32)
        mean = both[:, HEAD : 2 * HEAD] / width
        square = jnp.zeros((step_rows, HEAD), F32)
        for h in range(local):
            centred = hid[:, h * HEAD : (h + 1) * HEAD].astype(F32) - mean
            square = square + centred * centred
        spread2 = jnp.broadcast_to(jnp.sum(square, axis=-1, keepdims=True), (step_rows, HEAD))
        partial = both[:, 0:HEAD] - mean * col_src[0:1, :]

        def parts(x, count):
            out = []
            for _ in range(count):
                out.append(x.astype(BF16).astype(F32))
                x = x - out[-1]
            return out

        hi, lo = parts(partial, 2)
        sent = jnp.where(out_lane < half, hi, lo)
        for i, stat in enumerate((*parts(mean, 3), *parts(spread2, 2))):
            sent = jnp.where(out_lane == HEAD - 5 + i, stat, sent)
        for i, d in enumerate(pair_of):
            block = sent[i * pair_rows : (i + 1) * pair_rows].reshape(2, rows, HEAD)
            p_src[d] = block.astype(BF16)
            for x in (0, 1):
                move(R, d, x, p_src.at[d, core(x)], p_dst.at[c, z])

    for d in RING:
        arrived_col = pltpu.make_async_copy(col_src, col_dst.at[chip(n - d)], col_recv.at[d])
        arrived_col.wait()
    for d, x in everyone:
        arrived(R, d, x, p_dst.at[core(x), chip(n - d)])
    pick_row = lax.broadcasted_iota(jnp.int32, (HEAD, HEAD), 0)
    pick_col = lax.broadcasted_iota(jnp.int32, (HEAD, HEAD), 1)
    in_sum = (pick_row < HEAD - 5) & (lax.rem(pick_row, half) == lax.rem(pick_col, half))
    in_mean = (pick_row >= HEAD - 5) & (pick_row < HEAD - 2)
    in_square = pick_row >= HEAD - 2
    picks = [jnp.where(m, 1.0, 0.0).astype(BF16) for m in (in_sum, in_mean, in_square)]
    velocity = []
    for b in range(2):
        got = p_dst[b].astype(F32).reshape(n * rows, HEAD).astype(BF16)
        sums, means, squares = [
            jnp.dot(got, m, preferred_element_type=F32).reshape(n, rows, HEAD) for m in picks
        ]
        mean = jnp.sum(means, axis=0) / n
        away = means - mean[None]
        variance = (jnp.sum(squares, axis=0) + width * jnp.sum(away * away, axis=0)) / (heads * HEAD)
        total = jnp.zeros((rows, HEAD), F32)
        for s in range(n):
            total = total + (sums[s] + away[s] * col_dst[s, 0:1, :])
        velocity.append(total * lax.rsqrt(variance + NORM_EPS))
    guide = jnp.where(e == 0, HIGH_GUIDE, LOW_GUIDE)
    guided = (velocity[1] + guide * (velocity[0] - velocity[1]))[:, 0:half]
    now = jnp.full((rows, half), step[0, 0], jnp.int32).astype(F32)
    sigma_now = sigma_at(now)
    sigma_next = sigma_at(now + 1.0)
    step_v[...] = (lat[...] + (sigma_next - sigma_now) * guided).astype(BF16)
    copy = pltpu.make_async_remote_copy(
        step_v, hlat_out.at[0], x_send.at[2], x_recv.at[2], device_id={"expert": 1 - e}, device_id_type=MESH
    )
    copy.start()
    handed.append(copy)
    clean_v[...] = lat[...] - sigma_now * guided
    done = pltpu.make_async_copy(clean_v, clean_out.at[0], out_sem)
    done.start()
    for copy in sends:
        copy.wait_send()
    done.wait()
    for copy in handed:
        copy.wait()


def per_device(n, *args):
    queries, text_keys, latent, head_weight = args[0], args[7], args[11], args[12]
    rows, features = queries.shape[2:]
    heads = features // HEAD
    local = heads // n
    text, width = text_keys.shape[2:]
    channels = latent.shape[2]
    tokens = 2 * n * rows

    def kernel(*refs):
        body(n, rows, heads, *refs)

    anywhere = pl.BlockSpec(memory_space=pl.ANY)
    raw = pltpu.VMEM((2, rows, features), BF16)
    gain = pltpu.VMEM((1, features), F32)
    source = pltpu.VMEM((2, heads, rows, HEAD), BF16)
    landed = pltpu.VMEM((local, n, 2, rows, HEAD), BF16)
    merged = pltpu.VMEM((local, tokens, HEAD), BF16)
    dma = pltpu.SemaphoreType.DMA
    return pl.pallas_call(
        kernel,
        out_shape=(
            jax.ShapeDtypeStruct(latent.shape, F32),
            jax.ShapeDtypeStruct(latent.shape, BF16),
            jax.ShapeDtypeStruct(text_keys.shape, BF16),
            jax.ShapeDtypeStruct(text_keys.shape, BF16),
        ),
        in_specs=[anywhere] * len(args),
        out_specs=(anywhere,) * 4,
        scratch_shapes=[
            raw, raw, raw, gain, gain, gain,
            pltpu.VMEM((text, width), BF16), pltpu.VMEM((text, width), BF16),
            pltpu.SMEM((1, 1, 1), jnp.int32), pltpu.SMEM((1, 1), jnp.int32),
            pltpu.VMEM((rows, channels), F32), pltpu.VMEM((width, channels), BF16),
            source, source, source,
            pltpu.VMEM((n, 2, rows, width), BF16), landed, landed, landed,
            merged, merged, merged,
            pltpu.VMEM((local, tokens, 2 * HEAD), BF16), pltpu.VMEM((local, text, 2 * HEAD), BF16),
            pltpu.VMEM((local, tokens, HEAD), F32), pltpu.VMEM((4 * rows, width), BF16),
            pltpu.VMEM((rows, HEAD), F32), pltpu.VMEM((rows, HEAD), F32),
            pltpu.VMEM((text, width), BF16), pltpu.VMEM((text, width), BF16),
            pltpu.VMEM((width, 2 * HEAD), BF16), pltpu.VMEM((8, HEAD), F32), pltpu.VMEM((n, 8, HEAD), F32),
            pltpu.VMEM((n, 2, rows, HEAD), BF16), pltpu.VMEM((2, n, rows, HEAD), BF16),
            pltpu.VMEM((rows, channels), F32), pltpu.VMEM((rows, channels), BF16),
            dma((12,)), dma((5, n, 2)), dma((5, n, 2)), dma((n,)), dma((n,)), dma((3,)), dma((3,)), dma,
        ],
        compiler_params=pltpu.CompilerParams(
            collective_id=0, has_side_effects=True, vmem_limit_bytes=60 * 1024 * 1024
        ),
        cost_estimate=pl.CostEstimate(
            flops=1_000_000_000, bytes_accessed=4_000_000, transcendentals=2_000_000
        ),
    )(*args)


def solution(mesh):
    token_spec = P("expert", None, ("rep", "cfg", "sp"), None)
    text_spec = P("expert", "cfg", "rep", "sp")
    latent_spec = P("expert", ("rep", "cfg", "sp"), None)
    gain_spec = P("expert", None)
    in_specs = (
        *(token_spec,) * 4,
        *(gain_spec,) * 3,
        text_spec,
        text_spec,
        P("expert", "cfg", "rep"),
        P("expert", "rep"),
        latent_spec,
        P("expert", "sp", None),
    )
    out_specs = (latent_spec, latent_spec, text_spec, text_spec)
    count = mesh.shape["sp"]

    def run(*args):
        return per_device(count, *args)

    return jax.shard_map(run, mesh=mesh, in_specs=in_specs, out_specs=out_specs, check_vma=False)
```

```python
import math

import jax
import jax.numpy as jnp
from jax import lax
from jax.experimental import pallas as pl
from jax.experimental.pallas import tpu as pltpu
from jax.sharding import PartitionSpec as P

HEAD = 128
STEPS = 40
TIME_SHIFT = 12.0
HIGH_GUIDE = 4.0
LOW_GUIDE = 3.0
NORM_EPS = 1e-06

MESH = pl.DeviceIdType.MESH
BF16 = jnp.bfloat16
F32 = jnp.float32
RING = (4, 3, 5, 2, 6, 1, 7)
V, K, Q, C, R = range(5)


def sigma_at(index):
    frac = 1.0 - index / STEPS
    return TIME_SHIFT * frac / (1.0 + (TIME_SHIFT - 1.0) * frac)


def contract_last(a, b):
    return lax.dot_general(a, b, (((1,), (1,)), ((), ())), preferred_element_type=F32)


def body(n, rows, heads, *refs):
    (
        q_hbm, k_hbm, v_hbm, c_hbm, qg_hbm, kg_hbm, cg_hbm, tk_hbm, tv_hbm, len_hbm, step_hbm, lat_hbm, w_hbm,
        clean_out, hlat_out, hk_out, hv_out,
        q_in, k_in, c_in, qg, kg, cg, tk, tv, length, step, lat, w_in,
        q_src, k_src, c_src, v_dst, k_dst, q_dst, c_dst,
        kr, qr, cr, vr, self_o, hid, cos_t, sin_t,
        tk_m, tv_m, wcat, col_src, col_dst, p_src, p_dst, clean_v, step_v,
        load_sem, send_sem, recv_sem, col_send, col_recv, x_send, x_recv, out_sem,
    ) = refs
    local = heads // n
    width = local * HEAD
    e = lax.axis_index("expert")
    c = lax.axis_index("cfg")
    z = lax.axis_index("sp")

    def chip(d):
        return lax.rem(z + d, n)

    def core(x):
        return lax.rem(c + x, 2)

    remote = [(d, x) for d in RING for x in (0, 1)] + [(0, 1)]

    barrier = pltpu.get_barrier_semaphore()
    for d, x in remote:
        pl.semaphore_signal(barrier, 1, device_id={"cfg": core(x), "sp": chip(d)}, device_id_type=MESH)
    pl.semaphore_signal(barrier, 1, device_id={"expert": 1 - e}, device_id_type=MESH)

    loads = []
    for i, (src, dst) in enumerate(
        (
            (k_hbm.at[0], k_in), (kg_hbm, kg), (q_hbm.at[0], q_in), (qg_hbm, qg), (c_hbm.at[0], c_in), (cg_hbm, cg),
            (tk_hbm.at[0, 0], tk), (tv_hbm.at[0, 0], tv), (len_hbm, length), (step_hbm, step), (lat_hbm.at[0], lat),
            (w_hbm.at[0], w_in),
        )
    ):
        copy = pltpu.make_async_copy(src, dst, load_sem.at[i])
        copy.start()
        loads.append(copy)

    sends = []

    def move(a, d, x, src, dst):
        if (d, x) == (0, 0):
            copy = pltpu.make_async_copy(src, dst, recv_sem.at[a, 0, 0])
            copy.start()
            return
        copy = pltpu.make_async_remote_copy(
            src, dst, send_sem.at[a, d, x], recv_sem.at[a, d, x],
            device_id={"cfg": core(x), "sp": chip(d)}, device_id_type=MESH,
        )
        copy.start()
        sends.append(copy)

    def arrived(a, d, x, ref):
        pltpu.make_async_copy(ref, ref, recv_sem.at[a, d, x]).wait()

    def v_move(d, x):
        cols = pl.ds(pl.multiple_of(chip(d) * width, HEAD), width)
        move(V, d, x, v_hbm.at[0, core(x), :, cols], v_dst.at[z, c])

    v_move(0, 0)
    pl.semaphore_wait(barrier, len(remote) + 1)
    for d, x in remote:
        v_move(d, x)

    lane = lax.broadcasted_iota(jnp.int32, (rows, HEAD), 1)
    even = lax.rem(lane, 2) == 0
    row = lax.broadcasted_iota(jnp.int32, (rows, HEAD), 0)
    position = ((c * n + z) * rows + row).astype(F32)
    pair = (lane // 2).astype(F32)
    angle = position * jnp.exp(-(2.0 * pair / HEAD) * math.log(10000.0))
    cos_t[...] = jnp.cos(angle)
    sin = jnp.sin(angle)
    sin_t[...] = jnp.where(even, -sin, sin)

    def prepare(x_ref, g_ref, o_ref, rope):
        for b in range(2):

            def square(i, total):
                for j in range(local):
                    cols = pl.ds(pl.multiple_of(i * width + j * HEAD, HEAD), HEAD)
                    x = x_ref[b, :, cols].astype(F32)
                    total = total + x * x
                return total

            total = lax.fori_loop(0, n, square, jnp.zeros((rows, HEAD), F32))
            scale = lax.rsqrt(jnp.sum(total, axis=-1, keepdims=True) / (heads * HEAD) + NORM_EPS)

            def one(i, carry):
                for j in range(local):
                    cols = pl.ds(pl.multiple_of(i * width + j * HEAD, HEAD), HEAD)
                    x = x_ref[b, :, cols].astype(F32) * scale * g_ref[:, cols]
                    if rope:
                        partner = jnp.where(even, pltpu.roll(x, HEAD - 1, 1), pltpu.roll(x, 1, 1))
                        x = x * cos_t[...] + partner * sin_t[...]
                    o_ref[b, i * local + j] = x.astype(BF16)
                return carry

            lax.fori_loop(0, n, one, 0)

    def spread(a, src, dst):
        for d, x in [*remote, (0, 0)]:
            move(a, d, x, src.at[core(x), pl.ds(chip(d) * local, local)], dst.at[:, z, c])

    loads[0].wait()
    loads[1].wait()
    prepare(k_in, kg, k_src, True)
    spread(K, k_src, k_dst)
    loads[2].wait()
    loads[3].wait()
    prepare(q_in, qg, q_src, True)
    spread(Q, q_src, q_dst)
    loads[4].wait()
    loads[5].wait()
    prepare(c_in, cg, c_src, False)
    spread(C, c_src, c_dst)

    for i in range(6, 12):
        loads[i].wait()
    count = length[0, 0, 0]
    text = tk.shape[0]
    keep = lax.broadcasted_iota(jnp.int32, (text, width), 0) < count
    tk_m[...] = jnp.where(keep, tk[...].astype(F32), 0.0).astype(BF16)
    tv_m[...] = jnp.where(keep, tv[...].astype(F32), 0.0).astype(BF16)
    handed = []
    for i, (src, dst) in enumerate(((tk_m, hk_out.at[0, 0]), (tv_m, hv_out.at[0, 0]))):
        copy = pltpu.make_async_remote_copy(
            src, dst, x_send.at[i], x_recv.at[i], device_id={"expert": 1 - e}, device_id_type=MESH
        )
        copy.start()
        handed.append(copy)

    half = HEAD // 2
    wcat[0:half, :] = w_in[...]
    wcat[half:HEAD, :] = w_in[...]
    wcat[HEAD : 2 * HEAD, :] = jnp.ones((HEAD, width), BF16)
    col_src[...] = contract_last(jnp.ones((8, width), BF16), wcat[0:HEAD, :])
    col_dst[z] = col_src[...]
    for d in RING:
        copy = pltpu.make_async_remote_copy(
            col_src, col_dst.at[z], col_send.at[d], col_recv.at[d], device_id={"sp": chip(d)}, device_id_type=MESH
        )
        copy.start()
        sends.append(copy)

    everyone = [(d, x) for d in (0, *RING) for x in (0, 1)]
    pair_rows = 2 * rows

    def start_of(d):
        return pl.multiple_of(chip(n - d) * pair_rows, pair_rows)

    def gather(a, dst, out, d):
        at = chip(n - d)
        for x in (0, 1):
            arrived(a, d, x, dst.at[at, core(x)] if a == V else dst.at[:, at, core(x)])
        for h in range(local):
            block = dst[at, :, :, h * HEAD : (h + 1) * HEAD] if a == V else dst[h, at]
            block = block.astype(F32).reshape(pair_rows, HEAD).astype(BF16)
            out[h, pl.ds(start_of(d), pair_rows), :] = block

    factor = math.log2(math.e) / math.sqrt(HEAD)

    def weights(s):
        exponent = jnp.exp2((s - jnp.max(s, axis=-1, keepdims=True)) * factor)
        return (exponent * (1.0 / jnp.sum(exponent, axis=-1, keepdims=True))).astype(BF16)

    for a, dst, out in ((V, v_dst, vr), (K, k_dst, kr), (Q, q_dst, qr)):
        for d in (0, *RING):
            gather(a, dst, out, d)
    step_rows = 2 * pair_rows
    blocks = n // 2
    for h in range(local):
        for r in range(blocks):
            part = slice(r * step_rows, (r + 1) * step_rows)
            p = weights(contract_last(qr[h, part, :], kr[h]))
            self_o[h, part, :] = jnp.dot(p, vr[h], preferred_element_type=F32)

    used = lax.broadcasted_iota(jnp.int32, (step_rows, text), 1) < count
    out_lane = lax.broadcasted_iota(jnp.int32, (step_rows, HEAD), 1)
    order = (0, *RING)
    for r in range(blocks):
        pair_of = order[2 * r : 2 * r + 2]
        for d in pair_of:
            gather(C, c_dst, cr, d)
        starts = [start_of(d) for d in pair_of]

        def take(ref, h):
            return jnp.concatenate([ref[h, pl.ds(start, pair_rows), :] for start in starts], axis=0)

        for h in range(local):
            s = contract_last(take(cr, h), tk[:, h * HEAD : (h + 1) * HEAD])
            s = jnp.where(used, s, -jnp.inf)
            o = jnp.dot(weights(s), tv[:, h * HEAD : (h + 1) * HEAD], preferred_element_type=F32)
            hid[:, h * HEAD : (h + 1) * HEAD] = (take(self_o, h) + o).astype(BF16)
        both = contract_last(hid[...], wcat[...])
        mean = both[:, HEAD : 2 * HEAD] / width
        square = jnp.zeros((step_rows, HEAD), F32)
        for h in range(local):
            centred = hid[:, h * HEAD : (h + 1) * HEAD].astype(F32) - mean
            square = square + centred * centred
        spread2 = jnp.broadcast_to(jnp.sum(square, axis=-1, keepdims=True), (step_rows, HEAD))
        partial = both[:, 0:HEAD] - mean * col_src[0:1, :]

        def parts(x, count):
            out = []
            for _ in range(count):
                out.append(x.astype(BF16).astype(F32))
                x = x - out[-1]
            return out

        hi, lo = parts(partial, 2)
        sent = jnp.where(out_lane < half, hi, lo)
        for i, stat in enumerate((*parts(mean, 3), *parts(spread2, 2))):
            sent = jnp.where(out_lane == HEAD - 5 + i, stat, sent)
        for i, d in enumerate([(n - d) % n for d in pair_of]):
            block = sent[i * pair_rows : (i + 1) * pair_rows].reshape(2, rows, HEAD)
            p_src[d] = block.astype(BF16)
            for x in (0, 1):
                move(R, d, x, p_src.at[d, core(x)], p_dst.at[c, z])

    for d in RING:
        arrived_col = pltpu.make_async_copy(col_src, col_dst.at[chip(n - d)], col_recv.at[d])
        arrived_col.wait()
    for d, x in everyone:
        arrived(R, d, x, p_dst.at[core(x), chip(n - d)])
    pick_row = lax.broadcasted_iota(jnp.int32, (HEAD, HEAD), 0)
    pick_col = lax.broadcasted_iota(jnp.int32, (HEAD, HEAD), 1)
    in_sum = (pick_row < HEAD - 5) & (lax.rem(pick_row, half) == lax.rem(pick_col, half))
    in_mean = (pick_row >= HEAD - 5) & (pick_row < HEAD - 2)
    in_square = pick_row >= HEAD - 2
    picks = [jnp.where(m, 1.0, 0.0).astype(BF16) for m in (in_sum, in_mean, in_square)]
    velocity = []
    for b in range(2):
        got = p_dst[b].astype(F32).reshape(n * rows, HEAD).astype(BF16)
        sums, means, squares = [
            jnp.dot(got, m, preferred_element_type=F32).reshape(n, rows, HEAD) for m in picks
        ]
        mean = jnp.sum(means, axis=0) / n
        away = means - mean[None]
        variance = (jnp.sum(squares, axis=0) + width * jnp.sum(away * away, axis=0)) / (heads * HEAD)
        total = jnp.zeros((rows, HEAD), F32)
        for s in range(n):
            total = total + (sums[s] + away[s] * col_dst[s, 0:1, :])
        velocity.append(total * lax.rsqrt(variance + NORM_EPS))
    guide = jnp.where(e == 0, HIGH_GUIDE, LOW_GUIDE)
    guided = (velocity[1] + guide * (velocity[0] - velocity[1]))[:, 0:half]
    now = jnp.full((rows, half), step[0, 0], jnp.int32).astype(F32)
    sigma_now = sigma_at(now)
    sigma_next = sigma_at(now + 1.0)
    step_v[...] = (lat[...] + (sigma_next - sigma_now) * guided).astype(BF16)
    copy = pltpu.make_async_remote_copy(
        step_v, hlat_out.at[0], x_send.at[2], x_recv.at[2], device_id={"expert": 1 - e}, device_id_type=MESH
    )
    copy.start()
    handed.append(copy)
    clean_v[...] = lat[...] - sigma_now * guided
    done = pltpu.make_async_copy(clean_v, clean_out.at[0], out_sem)
    done.start()
    for copy in sends:
        copy.wait_send()
    done.wait()
    for copy in handed:
        copy.wait()


def hand_on(*refs):
    sem = refs[-1]
    arrive = [pltpu.make_async_copy(refs[i], refs[8 + i], sem.at[0, i]) for i in range(4)]
    leave = [pltpu.make_async_copy(refs[8 + i], refs[4 + i], sem.at[1, i]) for i in range(4)]
    for copy in arrive:
        copy.start()
    for i in range(4):
        arrive[i].wait()
        leave[i].start()
    for copy in leave:
        copy.wait()


def per_device(n, *args):
    queries, text_keys, latent = args[0], args[7], args[11]
    args = (*args[:12], jnp.swapaxes(args[12], 1, 2))
    rows, features = queries.shape[2:]
    heads = features // HEAD
    local = heads // n
    text, width = text_keys.shape[2:]
    channels = latent.shape[2]
    tokens = 2 * n * rows

    def kernel(*refs):
        body(n, rows, heads, *refs)

    anywhere = pl.BlockSpec(memory_space=pl.ANY)
    raw = pltpu.VMEM((2, rows, features), BF16)
    gain = pltpu.VMEM((1, features), F32)
    source = pltpu.VMEM((2, heads, rows, HEAD), BF16)
    landed = pltpu.VMEM((local, n, 2, rows, HEAD), BF16)
    merged = pltpu.VMEM((local, tokens, HEAD), BF16)
    dma = pltpu.SemaphoreType.DMA
    results = pl.pallas_call(
        kernel,
        out_shape=(
            jax.ShapeDtypeStruct(latent.shape, F32),
            jax.ShapeDtypeStruct(latent.shape, BF16),
            jax.ShapeDtypeStruct(text_keys.shape, BF16),
            jax.ShapeDtypeStruct(text_keys.shape, BF16),
        ),
        in_specs=[anywhere] * len(args),
        out_specs=(anywhere,) * 4,
        scratch_shapes=[
            raw, raw, raw, gain, gain, gain,
            pltpu.VMEM((text, width), BF16), pltpu.VMEM((text, width), BF16),
            pltpu.SMEM((1, 1, 1), jnp.int32), pltpu.SMEM((1, 1), jnp.int32),
            pltpu.VMEM((rows, channels), F32), pltpu.VMEM((channels, width), BF16),
            source, source, source,
            pltpu.VMEM((n, 2, rows, width), BF16), landed, landed, landed,
            merged, merged, merged, merged,
            pltpu.VMEM((local, tokens, HEAD), F32), pltpu.VMEM((4 * rows, width), BF16),
            pltpu.VMEM((rows, HEAD), F32), pltpu.VMEM((rows, HEAD), F32),
            pltpu.VMEM((text, width), BF16), pltpu.VMEM((text, width), BF16),
            pltpu.VMEM((2 * HEAD, width), BF16), pltpu.VMEM((8, HEAD), F32), pltpu.VMEM((n, 8, HEAD), F32),
            pltpu.VMEM((n, 2, rows, HEAD), BF16), pltpu.VMEM((2, n, rows, HEAD), BF16),
            pltpu.VMEM((rows, channels), F32), pltpu.VMEM((rows, channels), BF16),
            dma((12,)), dma((5, n, 2)), dma((5, n, 2)), dma((n,)), dma((n,)), dma((3,)), dma((3,)), dma,
        ],
        compiler_params=pltpu.CompilerParams(
            collective_id=0, has_side_effects=True, vmem_limit_bytes=60 * 1024 * 1024
        ),
        cost_estimate=pl.CostEstimate(
            flops=1_000_000_000, bytes_accessed=4_000_000, transcendentals=2_000_000
        ),
    )(*args)
    return pl.pallas_call(
        hand_on,
        out_shape=tuple(jax.ShapeDtypeStruct(r.shape, r.dtype) for r in results),
        in_specs=[anywhere] * 4,
        out_specs=(anywhere,) * 4,
        scratch_shapes=[*(pltpu.VMEM(r.shape, r.dtype) for r in results), dma((2, 4))],
        compiler_params=pltpu.CompilerParams(vmem_limit_bytes=60 * 1024 * 1024),
    )(*results)


def solution(mesh):
    token_spec = P("expert", None, ("rep", "cfg", "sp"), None)
    text_spec = P("expert", "cfg", "rep", "sp")
    latent_spec = P("expert", ("rep", "cfg", "sp"), None)
    gain_spec = P("expert", None)
    in_specs = (
        *(token_spec,) * 4,
        *(gain_spec,) * 3,
        text_spec,
        text_spec,
        P("expert", "cfg", "rep"),
        P("expert", "rep"),
        latent_spec,
        P("expert", "sp", None),
    )
    out_specs = (latent_spec, latent_spec, text_spec, text_spec)
    count = mesh.shape["sp"]

    def run(*args):
        return per_device(count, *args)

    return jax.shard_map(run, mesh=mesh, in_specs=in_specs, out_specs=out_specs, check_vma=False)
```

```python
import math

import jax
import jax.numpy as jnp
from jax import lax
from jax.experimental import pallas as pl
from jax.experimental.pallas import tpu as pltpu
from jax.sharding import PartitionSpec as P

HEAD = 128
STEPS = 40
TIME_SHIFT = 12.0
HIGH_GUIDE = 4.0
LOW_GUIDE = 3.0
NORM_EPS = 1e-06

MESH = pl.DeviceIdType.MESH
BF16 = jnp.bfloat16
F32 = jnp.float32
RING = (4, 3, 5, 2, 6, 1, 7)
V, K, Q, C, R = range(5)


def sigma_at(index):
    frac = 1.0 - index / STEPS
    return TIME_SHIFT * frac / (1.0 + (TIME_SHIFT - 1.0) * frac)


def contract_last(a, b):
    return lax.dot_general(a, b, (((1,), (1,)), ((), ())), preferred_element_type=F32)


def body(n, rows, heads, *refs):
    (
        q_hbm, k_hbm, v_hbm, c_hbm, qg_hbm, kg_hbm, cg_hbm, tk_hbm, tv_hbm, len_hbm, step_hbm, lat_hbm, w_hbm,
        clean_out, hlat_out, hk_out, hv_out,
        q_in, k_in, c_in, qg, kg, cg, tk, tv, length, step, lat, w_in,
        q_src, k_src, c_src, v_dst, k_dst, q_dst, c_dst,
        kr, qr, cr, vr, self_o, hid, cos_t, sin_t,
        tk_m, tv_m, wcat, col_src, col_dst, p_src, p_dst, clean_v, step_v,
        load_sem, send_sem, recv_sem, col_send, col_recv, x_send, x_recv, out_sem,
    ) = refs
    local = heads // n
    width = local * HEAD
    e = lax.axis_index("expert")
    c = lax.axis_index("cfg")
    z = lax.axis_index("sp")

    def chip(d):
        return lax.rem(z + d, n)

    def core(x):
        return lax.rem(c + x, 2)

    remote = [(d, x) for d in RING for x in (0, 1)] + [(0, 1)]

    barrier = pltpu.get_barrier_semaphore()
    for d, x in remote:
        pl.semaphore_signal(barrier, 1, device_id={"cfg": core(x), "sp": chip(d)}, device_id_type=MESH)
    pl.semaphore_signal(barrier, 1, device_id={"expert": 1 - e}, device_id_type=MESH)

    loads = []
    for i, (src, dst) in enumerate(
        (
            (k_hbm.at[0], k_in), (kg_hbm, kg), (q_hbm.at[0], q_in), (qg_hbm, qg), (c_hbm.at[0], c_in), (cg_hbm, cg),
            (tk_hbm.at[0, 0], tk), (tv_hbm.at[0, 0], tv), (len_hbm, length), (step_hbm, step), (lat_hbm.at[0], lat),
            (w_hbm.at[0], w_in),
        )
    ):
        copy = pltpu.make_async_copy(src, dst, load_sem.at[i])
        copy.start()
        loads.append(copy)

    sends = []

    def move(a, d, x, src, dst):
        if (d, x) == (0, 0):
            copy = pltpu.make_async_copy(src, dst, recv_sem.at[a, 0, 0])
            copy.start()
            return
        copy = pltpu.make_async_remote_copy(
            src, dst, send_sem.at[a, d, x], recv_sem.at[a, d, x],
            device_id={"cfg": core(x), "sp": chip(d)}, device_id_type=MESH,
        )
        copy.start()
        sends.append(copy)

    def arrived(a, d, x, ref):
        pltpu.make_async_copy(ref, ref, recv_sem.at[a, d, x]).wait()

    def v_move(d, x):
        cols = pl.ds(pl.multiple_of(chip(d) * width, HEAD), width)
        move(V, d, x, v_hbm.at[0, core(x), :, cols], v_dst.at[z, c])

    v_move(0, 0)
    pl.semaphore_wait(barrier, len(remote) + 1)
    for d, x in remote:
        v_move(d, x)

    lane = lax.broadcasted_iota(jnp.int32, (rows, HEAD), 1)
    even = lax.rem(lane, 2) == 0
    row = lax.broadcasted_iota(jnp.int32, (rows, HEAD), 0)
    position = ((c * n + z) * rows + row).astype(F32)
    pair = (lane // 2).astype(F32)
    angle = position * jnp.exp(-(2.0 * pair / HEAD) * math.log(10000.0))
    cos_t[...] = jnp.cos(angle)
    sin = jnp.sin(angle)
    sin_t[...] = jnp.where(even, -sin, sin)

    def prepare(x_ref, g_ref, o_ref, rope):
        for b in range(2):

            def square(i, total):
                for j in range(local):
                    cols = pl.ds(pl.multiple_of(i * width + j * HEAD, HEAD), HEAD)
                    x = x_ref[b, :, cols].astype(F32)
                    total = total + x * x
                return total

            total = lax.fori_loop(0, n, square, jnp.zeros((rows, HEAD), F32))
            scale = lax.rsqrt(jnp.sum(total, axis=-1, keepdims=True) / (heads * HEAD) + NORM_EPS)

            def one(i, carry):
                for j in range(local):
                    cols = pl.ds(pl.multiple_of(i * width + j * HEAD, HEAD), HEAD)
                    x = x_ref[b, :, cols].astype(F32) * scale * g_ref[:, cols]
                    if rope:
                        partner = jnp.where(even, pltpu.roll(x, HEAD - 1, 1), pltpu.roll(x, 1, 1))
                        x = x * cos_t[...] + partner * sin_t[...]
                    o_ref[b, i * local + j] = x.astype(BF16)
                return carry

            lax.fori_loop(0, n, one, 0)

    def spread(a, src, dst):
        for d, x in [*remote, (0, 0)]:
            move(a, d, x, src.at[core(x), pl.ds(chip(d) * local, local)], dst.at[:, z, c])

    loads[0].wait()
    loads[1].wait()
    prepare(k_in, kg, k_src, True)
    spread(K, k_src, k_dst)
    loads[2].wait()
    loads[3].wait()
    prepare(q_in, qg, q_src, True)
    spread(Q, q_src, q_dst)
    loads[4].wait()
    loads[5].wait()
    prepare(c_in, cg, c_src, False)
    spread(C, c_src, c_dst)

    for i in range(6, 12):
        loads[i].wait()
    count = length[0, 0, 0]
    text = tk.shape[0]
    keep = lax.broadcasted_iota(jnp.int32, (text, width), 0) < count
    tk_m[...] = jnp.where(keep, tk[...].astype(F32), 0.0).astype(BF16)
    tv_m[...] = jnp.where(keep, tv[...].astype(F32), 0.0).astype(BF16)
    handed = []
    for i, (src, dst) in enumerate(((tk_m, hk_out.at[0, 0]), (tv_m, hv_out.at[0, 0]))):
        copy = pltpu.make_async_remote_copy(
            src, dst, x_send.at[i], x_recv.at[i], device_id={"expert": 1 - e}, device_id_type=MESH
        )
        copy.start()
        handed.append(copy)

    half = HEAD // 2
    wcat[0:half, :] = w_in[...]
    wcat[half:HEAD, :] = w_in[...]
    wcat[HEAD : 2 * HEAD, :] = jnp.ones((HEAD, width), BF16)
    col_src[...] = contract_last(jnp.ones((8, width), BF16), wcat[0:HEAD, :])[0:1]
    col_dst[z] = col_src[...]
    for d in RING:
        copy = pltpu.make_async_remote_copy(
            col_src, col_dst.at[z], col_send.at[d], col_recv.at[d], device_id={"sp": chip(d)}, device_id_type=MESH
        )
        copy.start()
        sends.append(copy)

    everyone = [(d, x) for d in (0, *RING) for x in (0, 1)]
    pair_rows = 2 * rows

    def start_of(d):
        return pl.multiple_of(chip(n - d) * pair_rows, pair_rows)

    def gather(a, dst, out, d):
        at = chip(n - d)
        for x in (0, 1):
            arrived(a, d, x, dst.at[at, core(x)] if a == V else dst.at[:, at, core(x)])
        for h in range(local):
            block = dst[at, :, :, h * HEAD : (h + 1) * HEAD] if a == V else dst[h, at]
            block = block.astype(F32).reshape(pair_rows, HEAD).astype(BF16)
            out[h, pl.ds(start_of(d), pair_rows), :] = block

    factor = math.log2(math.e) / math.sqrt(HEAD)

    def weights(s):
        exponent = jnp.exp2((s - jnp.max(s, axis=-1, keepdims=True)) * factor)
        return (exponent * (1.0 / jnp.sum(exponent, axis=-1, keepdims=True))).astype(BF16)

    for a, dst, out in ((V, v_dst, vr), (K, k_dst, kr), (Q, q_dst, qr)):
        for d in (0, *RING):
            gather(a, dst, out, d)
    step_rows = 2 * pair_rows
    blocks = n // 2
    for h in range(local):
        for r in range(blocks):
            part = slice(r * step_rows, (r + 1) * step_rows)
            p = weights(contract_last(qr[h, part, :], kr[h]))
            self_o[h, part, :] = jnp.dot(p, vr[h], preferred_element_type=F32)

    used = lax.broadcasted_iota(jnp.int32, (step_rows, text), 1) < count
    out_lane = lax.broadcasted_iota(jnp.int32, (step_rows, HEAD), 1)
    order = (0, *RING)
    for r in range(blocks):
        pair_of = order[2 * r : 2 * r + 2]
        for d in pair_of:
            gather(C, c_dst, cr, d)
        starts = [start_of(d) for d in pair_of]

        def take(ref, h):
            return jnp.concatenate([ref[h, pl.ds(start, pair_rows), :] for start in starts], axis=0)

        for h in range(local):
            s = contract_last(take(cr, h), tk[:, h * HEAD : (h + 1) * HEAD])
            s = jnp.where(used, s, -jnp.inf)
            o = jnp.dot(weights(s), tv[:, h * HEAD : (h + 1) * HEAD], preferred_element_type=F32)
            hid[:, h * HEAD : (h + 1) * HEAD] = (take(self_o, h) + o).astype(BF16)
        both = contract_last(hid[...], wcat[...])
        mean = both[:, HEAD : 2 * HEAD] / width
        square = jnp.zeros((step_rows, HEAD), F32)
        for h in range(local):
            centred = hid[:, h * HEAD : (h + 1) * HEAD].astype(F32) - mean
            square = square + centred * centred
        spread2 = jnp.broadcast_to(jnp.sum(square, axis=-1, keepdims=True), (step_rows, HEAD))
        partial = both[:, 0:HEAD] - mean * col_src[0:1, :]

        def parts(x, count):
            out = []
            for _ in range(count):
                out.append(x.astype(BF16).astype(F32))
                x = x - out[-1]
            return out

        hi, lo = parts(partial, 2)
        sent = jnp.where(out_lane < half, hi, lo)
        for i, stat in enumerate((*parts(mean, 3), *parts(spread2, 2))):
            sent = jnp.where(out_lane == HEAD - 5 + i, stat, sent)
        for i, d in enumerate([(n - d) % n for d in pair_of]):
            block = sent[i * pair_rows : (i + 1) * pair_rows].reshape(2, rows, HEAD)
            p_src[d] = block.astype(BF16)
            for x in (0, 1):
                move(R, d, x, p_src.at[d, core(x)], p_dst.at[c, z])

    for d in RING:
        arrived_col = pltpu.make_async_copy(col_src, col_dst.at[chip(n - d)], col_recv.at[d])
        arrived_col.wait()
    for d, x in everyone:
        arrived(R, d, x, p_dst.at[core(x), chip(n - d)])
    pick_row = lax.broadcasted_iota(jnp.int32, (HEAD, HEAD), 0)
    pick_col = lax.broadcasted_iota(jnp.int32, (HEAD, HEAD), 1)
    in_sum = (pick_row < HEAD - 5) & (lax.rem(pick_row, half) == lax.rem(pick_col, half))
    in_mean = (pick_row >= HEAD - 5) & (pick_row < HEAD - 2)
    in_square = pick_row >= HEAD - 2
    picks = [jnp.where(m, 1.0, 0.0).astype(BF16) for m in (in_sum, in_mean, in_square)]
    velocity = []
    for b in range(2):
        got = p_dst[b].astype(F32).reshape(n * rows, HEAD).astype(BF16)
        sums, means, squares = [
            jnp.dot(got, m, preferred_element_type=F32).reshape(n, rows, HEAD) for m in picks
        ]
        mean = jnp.sum(means, axis=0) / n
        away = means - mean[None]
        variance = (jnp.sum(squares, axis=0) + width * jnp.sum(away * away, axis=0)) / (heads * HEAD)
        total = jnp.zeros((rows, HEAD), F32)
        for s in range(n):
            total = total + (sums[s] + away[s] * col_dst[s, 0:1, :])
        velocity.append(total * lax.rsqrt(variance + NORM_EPS))
    guide = jnp.where(e == 0, HIGH_GUIDE, LOW_GUIDE)
    guided = (velocity[1] + guide * (velocity[0] - velocity[1]))[:, 0:half]
    now = jnp.full((rows, half), step[0, 0], jnp.int32).astype(F32)
    sigma_now = sigma_at(now)
    sigma_next = sigma_at(now + 1.0)
    step_v[...] = (lat[...] + (sigma_next - sigma_now) * guided).astype(BF16)
    copy = pltpu.make_async_remote_copy(
        step_v, hlat_out.at[0], x_send.at[2], x_recv.at[2], device_id={"expert": 1 - e}, device_id_type=MESH
    )
    copy.start()
    handed.append(copy)
    clean_v[...] = lat[...] - sigma_now * guided
    done = pltpu.make_async_copy(clean_v, clean_out.at[0], out_sem)
    done.start()
    for copy in sends:
        copy.wait_send()
    done.wait()
    for copy in handed:
        copy.wait()


def hand_on(*refs):
    sem = refs[-1]
    arrive = [pltpu.make_async_copy(refs[i], refs[8 + i], sem.at[0, i]) for i in range(4)]
    leave = [pltpu.make_async_copy(refs[8 + i], refs[4 + i], sem.at[1, i]) for i in range(4)]
    for copy in arrive:
        copy.start()
    for i in range(4):
        arrive[i].wait()
        leave[i].start()
    for copy in leave:
        copy.wait()


def per_device(n, *args):
    queries, text_keys, latent = args[0], args[7], args[11]
    args = (*args[:12], jnp.swapaxes(args[12], 1, 2))
    rows, features = queries.shape[2:]
    heads = features // HEAD
    local = heads // n
    text, width = text_keys.shape[2:]
    channels = latent.shape[2]
    tokens = 2 * n * rows

    def kernel(*refs):
        body(n, rows, heads, *refs)

    anywhere = pl.BlockSpec(memory_space=pl.ANY)
    raw = pltpu.VMEM((2, rows, features), BF16)
    gain = pltpu.VMEM((1, features), F32)
    source = pltpu.VMEM((2, heads, rows, HEAD), BF16)
    landed = pltpu.VMEM((local, n, 2, rows, HEAD), BF16)
    merged = pltpu.VMEM((local, tokens, HEAD), BF16)
    dma = pltpu.SemaphoreType.DMA
    results = pl.pallas_call(
        kernel,
        out_shape=(
            jax.ShapeDtypeStruct(latent.shape, F32),
            jax.ShapeDtypeStruct(latent.shape, BF16),
            jax.ShapeDtypeStruct(text_keys.shape, BF16),
            jax.ShapeDtypeStruct(text_keys.shape, BF16),
        ),
        in_specs=[anywhere] * len(args),
        out_specs=(anywhere,) * 4,
        scratch_shapes=[
            raw, raw, raw, gain, gain, gain,
            pltpu.VMEM((text, width), BF16), pltpu.VMEM((text, width), BF16),
            pltpu.SMEM((1, 1, 1), jnp.int32), pltpu.SMEM((1, 1), jnp.int32),
            pltpu.VMEM((rows, channels), F32), pltpu.VMEM((channels, width), BF16),
            source, source, source,
            pltpu.VMEM((n, 2, rows, width), BF16), landed, landed, landed,
            merged, merged, merged, merged,
            pltpu.VMEM((local, tokens, HEAD), F32), pltpu.VMEM((4 * rows, width), BF16),
            pltpu.VMEM((rows, HEAD), F32), pltpu.VMEM((rows, HEAD), F32),
            pltpu.VMEM((text, width), BF16), pltpu.VMEM((text, width), BF16),
            pltpu.VMEM((2 * HEAD, width), BF16), pltpu.VMEM((1, HEAD), F32), pltpu.VMEM((n, 1, HEAD), F32),
            pltpu.VMEM((n, 2, rows, HEAD), BF16), pltpu.VMEM((2, n, rows, HEAD), BF16),
            pltpu.VMEM((rows, channels), F32), pltpu.VMEM((rows, channels), BF16),
            dma((12,)), dma((5, n, 2)), dma((5, n, 2)), dma((n,)), dma((n,)), dma((3,)), dma((3,)), dma,
        ],
        compiler_params=pltpu.CompilerParams(
            collective_id=0, has_side_effects=True, vmem_limit_bytes=60 * 1024 * 1024
        ),
        cost_estimate=pl.CostEstimate(
            flops=1_000_000_000, bytes_accessed=4_000_000, transcendentals=2_000_000
        ),
    )(*args)
    return pl.pallas_call(
        hand_on,
        out_shape=tuple(jax.ShapeDtypeStruct(r.shape, r.dtype) for r in results),
        in_specs=[anywhere] * 4,
        out_specs=(anywhere,) * 4,
        scratch_shapes=[*(pltpu.VMEM(r.shape, r.dtype) for r in results), dma((2, 4))],
        compiler_params=pltpu.CompilerParams(vmem_limit_bytes=60 * 1024 * 1024),
    )(*results)


def solution(mesh):
    token_spec = P("expert", None, ("rep", "cfg", "sp"), None)
    text_spec = P("expert", "cfg", "rep", "sp")
    latent_spec = P("expert", ("rep", "cfg", "sp"), None)
    gain_spec = P("expert", None)
    in_specs = (
        *(token_spec,) * 4,
        *(gain_spec,) * 3,
        text_spec,
        text_spec,
        P("expert", "cfg", "rep"),
        P("expert", "rep"),
        latent_spec,
        P("expert", "sp", None),
    )
    out_specs = (latent_spec, latent_spec, text_spec, text_spec)
    count = mesh.shape["sp"]

    def run(*args):
        return per_device(count, *args)

    return jax.shard_map(run, mesh=mesh, in_specs=in_specs, out_specs=out_specs, check_vma=False)
```

```python
import math

import jax
import jax.numpy as jnp
from jax import lax
from jax.experimental import pallas as pl
from jax.experimental.pallas import tpu as pltpu
from jax.sharding import PartitionSpec as P

HEAD = 128
STEPS = 40
TIME_SHIFT = 12.0
HIGH_GUIDE = 4.0
LOW_GUIDE = 3.0
NORM_EPS = 1e-06

MESH = pl.DeviceIdType.MESH
BF16 = jnp.bfloat16
F32 = jnp.float32
RING = (4, 3, 5, 2, 6, 1, 7)
V, K, Q, C, R = range(5)


def sigma_at(index):
    frac = 1.0 - index / STEPS
    return TIME_SHIFT * frac / (1.0 + (TIME_SHIFT - 1.0) * frac)


def contract_last(a, b):
    return lax.dot_general(a, b, (((1,), (1,)), ((), ())), preferred_element_type=F32)


def body(n, rows, heads, *refs):
    (
        q_hbm, k_hbm, v_hbm, c_hbm, qg_hbm, kg_hbm, cg_hbm, tk_hbm, tv_hbm, len_hbm, step_hbm, lat_hbm, w_hbm,
        clean_out, hlat_out, hk_out, hv_out,
        q_in, k_in, c_in, qg, kg, cg, tk, tv, length, step, lat, w_in,
        q_src, k_src, c_src, v_dst, k_dst, q_dst, c_dst,
        kr, qr, cr, vr, self_o, hid, cos_t, sin_t,
        tk_m, tv_m, wcat, col_src, col_dst, p_src, p_dst, pick_ref, sigmas, clean_v, step_v,
        load_sem, send_sem, recv_sem, col_send, col_recv, x_send, x_recv, out_sem,
    ) = refs
    local = heads // n
    width = local * HEAD
    e = lax.axis_index("expert")
    c = lax.axis_index("cfg")
    z = lax.axis_index("sp")

    def chip(d):
        return lax.rem(z + d, n)

    def core(x):
        return lax.rem(c + x, 2)

    remote = [(d, x) for d in RING for x in (0, 1)] + [(0, 1)]

    barrier = pltpu.get_barrier_semaphore()
    for d, x in remote:
        pl.semaphore_signal(barrier, 1, device_id={"cfg": core(x), "sp": chip(d)}, device_id_type=MESH)
    pl.semaphore_signal(barrier, 1, device_id={"expert": 1 - e}, device_id_type=MESH)

    loads = []
    for i, (src, dst) in enumerate(
        (
            (k_hbm.at[0], k_in), (kg_hbm, kg), (q_hbm.at[0], q_in), (qg_hbm, qg), (c_hbm.at[0], c_in), (cg_hbm, cg),
            (tk_hbm.at[0, 0], tk), (tv_hbm.at[0, 0], tv), (len_hbm, length), (step_hbm, step), (lat_hbm.at[0], lat),
            (w_hbm.at[0], w_in),
        )
    ):
        copy = pltpu.make_async_copy(src, dst, load_sem.at[i])
        copy.start()
        loads.append(copy)

    sends = []

    def move(a, d, x, src, dst):
        if (d, x) == (0, 0):
            copy = pltpu.make_async_copy(src, dst, recv_sem.at[a, 0, 0])
            copy.start()
            return
        copy = pltpu.make_async_remote_copy(
            src, dst, send_sem.at[a, d, x], recv_sem.at[a, d, x],
            device_id={"cfg": core(x), "sp": chip(d)}, device_id_type=MESH,
        )
        copy.start()
        sends.append(copy)

    def arrived(a, d, x, ref):
        pltpu.make_async_copy(ref, ref, recv_sem.at[a, d, x]).wait()

    def v_move(d, x):
        cols = pl.ds(pl.multiple_of(chip(d) * width, HEAD), width)
        move(V, d, x, v_hbm.at[0, core(x), :, cols], v_dst.at[z, c])

    v_move(0, 0)
    pl.semaphore_wait(barrier, len(remote) + 1)
    for d, x in remote:
        v_move(d, x)

    lane = lax.broadcasted_iota(jnp.int32, (rows, HEAD), 1)
    even = lax.rem(lane, 2) == 0
    row = lax.broadcasted_iota(jnp.int32, (rows, HEAD), 0)
    position = ((c * n + z) * rows + row).astype(F32)
    pair = (lane // 2).astype(F32)
    angle = position * jnp.exp(-(2.0 * pair / HEAD) * math.log(10000.0))
    cos_t[...] = jnp.cos(angle)
    sin = jnp.sin(angle)
    sin_t[...] = jnp.where(even, -sin, sin)

    def prepare(x_ref, g_ref, o_ref, rope):
        for b in range(2):

            def square(i, total):
                for j in range(local):
                    cols = pl.ds(pl.multiple_of(i * width + j * HEAD, HEAD), HEAD)
                    x = x_ref[b, :, cols].astype(F32)
                    total = total + x * x
                return total

            total = lax.fori_loop(0, n, square, jnp.zeros((rows, HEAD), F32))
            scale = lax.rsqrt(jnp.sum(total, axis=-1, keepdims=True) / (heads * HEAD) + NORM_EPS)

            def one(i, carry):
                for j in range(local):
                    cols = pl.ds(pl.multiple_of(i * width + j * HEAD, HEAD), HEAD)
                    x = x_ref[b, :, cols].astype(F32) * scale * g_ref[:, cols]
                    if rope:
                        partner = jnp.where(even, pltpu.roll(x, HEAD - 1, 1), pltpu.roll(x, 1, 1))
                        x = x * cos_t[...] + partner * sin_t[...]
                    o_ref[b, i * local + j] = x.astype(BF16)
                return carry

            lax.fori_loop(0, n, one, 0)

    def spread(a, src, dst):
        for d, x in [*remote, (0, 0)]:
            move(a, d, x, src.at[core(x), pl.ds(chip(d) * local, local)], dst.at[:, z, c])

    loads[0].wait()
    loads[1].wait()
    prepare(k_in, kg, k_src, True)
    spread(K, k_src, k_dst)
    loads[2].wait()
    loads[3].wait()
    prepare(q_in, qg, q_src, True)
    spread(Q, q_src, q_dst)
    loads[4].wait()
    loads[5].wait()
    prepare(c_in, cg, c_src, False)
    spread(C, c_src, c_dst)

    for i in range(6, 12):
        loads[i].wait()
    count = length[0, 0, 0]
    text = tk.shape[0]
    keep = lax.broadcasted_iota(jnp.int32, (text, width), 0) < count
    tk_m[...] = jnp.where(keep, tk[...].astype(F32), 0.0).astype(BF16)
    tv_m[...] = jnp.where(keep, tv[...].astype(F32), 0.0).astype(BF16)
    handed = []
    for i, (src, dst) in enumerate(((tk_m, hk_out.at[0, 0]), (tv_m, hv_out.at[0, 0]))):
        copy = pltpu.make_async_remote_copy(
            src, dst, x_send.at[i], x_recv.at[i], device_id={"expert": 1 - e}, device_id_type=MESH
        )
        copy.start()
        handed.append(copy)

    half = HEAD // 2
    wcat[0:half, :] = w_in[...]
    wcat[half:HEAD, :] = w_in[...]
    wcat[HEAD : 2 * HEAD, :] = jnp.ones((HEAD, width), BF16)
    col_src[...] = contract_last(jnp.ones((8, width), BF16), wcat[0:HEAD, :])[0:1]
    col_dst[z] = col_src[...]
    for d in RING:
        copy = pltpu.make_async_remote_copy(
            col_src, col_dst.at[z], col_send.at[d], col_recv.at[d], device_id={"sp": chip(d)}, device_id_type=MESH
        )
        copy.start()
        sends.append(copy)

    everyone = [(d, x) for d in (0, *RING) for x in (0, 1)]
    pair_rows = 2 * rows

    def start_of(d):
        return pl.multiple_of(chip(n - d) * pair_rows, pair_rows)

    def gather(a, dst, out, d):
        at = chip(n - d)
        for x in (0, 1):
            arrived(a, d, x, dst.at[at, core(x)] if a == V else dst.at[:, at, core(x)])
        for h in range(local):
            block = dst[at, :, :, h * HEAD : (h + 1) * HEAD] if a == V else dst[h, at]
            block = block.astype(F32).reshape(pair_rows, HEAD).astype(BF16)
            out[h, pl.ds(start_of(d), pair_rows), :] = block

    factor = math.log2(math.e) / math.sqrt(HEAD)

    def weights(s):
        exponent = jnp.exp2((s - jnp.max(s, axis=-1, keepdims=True)) * factor)
        return (exponent * (1.0 / jnp.sum(exponent, axis=-1, keepdims=True))).astype(BF16)

    for a, dst, out in ((V, v_dst, vr), (K, k_dst, kr), (Q, q_dst, qr)):
        for d in (0, *RING):
            gather(a, dst, out, d)
    step_rows = 2 * pair_rows
    blocks = n // 2
    for h in range(local):
        for r in range(blocks):
            part = slice(r * step_rows, (r + 1) * step_rows)
            p = weights(contract_last(qr[h, part, :], kr[h]))
            self_o[h, part, :] = jnp.dot(p, vr[h], preferred_element_type=F32)

    used = lax.broadcasted_iota(jnp.int32, (step_rows, text), 1) < count
    out_lane = lax.broadcasted_iota(jnp.int32, (step_rows, HEAD), 1)
    order = (0, *RING)
    for r in range(blocks):
        pair_of = order[2 * r : 2 * r + 2]
        for d in pair_of:
            gather(C, c_dst, cr, d)
        starts = [start_of(d) for d in pair_of]

        def take(ref, h):
            return jnp.concatenate([ref[h, pl.ds(start, pair_rows), :] for start in starts], axis=0)

        for h in range(local):
            s = contract_last(take(cr, h), tk[:, h * HEAD : (h + 1) * HEAD])
            s = jnp.where(used, s, -jnp.inf)
            o = jnp.dot(weights(s), tv[:, h * HEAD : (h + 1) * HEAD], preferred_element_type=F32)
            hid[:, h * HEAD : (h + 1) * HEAD] = (take(self_o, h) + o).astype(BF16)
        both = contract_last(hid[...], wcat[...])
        mean = both[:, HEAD : 2 * HEAD] / width
        square = jnp.zeros((step_rows, HEAD), F32)
        for h in range(local):
            centred = hid[:, h * HEAD : (h + 1) * HEAD].astype(F32) - mean
            square = square + centred * centred
        spread2 = jnp.broadcast_to(jnp.sum(square, axis=-1, keepdims=True), (step_rows, HEAD))
        partial = both[:, 0:HEAD] - mean * col_src[0:1, :]

        def parts(x, count):
            out = []
            for _ in range(count):
                out.append(x.astype(BF16).astype(F32))
                x = x - out[-1]
            return out

        hi, lo = parts(partial, 2)
        sent = jnp.where(out_lane < half, hi, lo)
        for i, stat in enumerate((*parts(mean, 3), *parts(spread2, 2))):
            sent = jnp.where(out_lane == HEAD - 5 + i, stat, sent)
        for i, d in enumerate([(n - d) % n for d in pair_of]):
            block = sent[i * pair_rows : (i + 1) * pair_rows].reshape(2, rows, HEAD)
            p_src[d] = block.astype(BF16)
            for x in (0, 1):
                move(R, d, x, p_src.at[d, core(x)], p_dst.at[c, z])

    pick_row = lax.broadcasted_iota(jnp.int32, (HEAD, HEAD), 0)
    pick_col = lax.broadcasted_iota(jnp.int32, (HEAD, HEAD), 1)
    in_sum = (pick_row < HEAD - 5) & (lax.rem(pick_row, half) == lax.rem(pick_col, half))
    in_mean = (pick_row >= HEAD - 5) & (pick_row < HEAD - 2)
    in_square = pick_row >= HEAD - 2
    picks = [jnp.where(m, 1.0, 0.0).astype(BF16) for m in (in_sum, in_mean, in_square)]
    now = jnp.full((rows, half), step[0, 0], jnp.int32).astype(F32)
    sigmas[0] = sigma_at(now)
    sigmas[1] = sigma_at(now + 1.0)
    for i, m in enumerate(picks):
        pick_ref[i] = m
    for copy in sends[: 4 * len(remote) + len(RING)]:
        copy.wait_send()

    for d in RING:
        arrived_col = pltpu.make_async_copy(col_src, col_dst.at[chip(n - d)], col_recv.at[d])
        arrived_col.wait()
    for d, x in everyone:
        arrived(R, d, x, p_dst.at[core(x), chip(n - d)])
    velocity = []
    for b in range(2):
        got = p_dst[b].astype(F32).reshape(n * rows, HEAD).astype(BF16)
        sums, means, squares = [
            jnp.dot(got, m, preferred_element_type=F32).reshape(n, rows, HEAD) for m in (pick_ref[0], pick_ref[1], pick_ref[2])
        ]
        mean = jnp.sum(means, axis=0) / n
        away = means - mean[None]
        variance = (jnp.sum(squares, axis=0) + width * jnp.sum(away * away, axis=0)) / (heads * HEAD)
        total = jnp.zeros((rows, HEAD), F32)
        for s in range(n):
            total = total + (sums[s] + away[s] * col_dst[s, 0:1, :])
        velocity.append(total * lax.rsqrt(variance + NORM_EPS))
    sigma_now, sigma_next = sigmas[0], sigmas[1]
    guide = jnp.where(e == 0, HIGH_GUIDE, LOW_GUIDE)
    guided = (velocity[1] + guide * (velocity[0] - velocity[1]))[:, 0:half]
    step_v[...] = (lat[...] + (sigma_next - sigma_now) * guided).astype(BF16)
    copy = pltpu.make_async_remote_copy(
        step_v, hlat_out.at[0], x_send.at[2], x_recv.at[2], device_id={"expert": 1 - e}, device_id_type=MESH
    )
    copy.start()
    handed.append(copy)
    clean_v[...] = lat[...] - sigma_now * guided
    done = pltpu.make_async_copy(clean_v, clean_out.at[0], out_sem)
    done.start()
    for copy in sends[4 * len(remote) + len(RING) :]:
        copy.wait_send()
    done.wait()
    for copy in handed:
        copy.wait()


def hand_on(*refs):
    sem = refs[-1]
    arrive = [pltpu.make_async_copy(refs[i], refs[8 + i], sem.at[0, i]) for i in range(4)]
    leave = [pltpu.make_async_copy(refs[8 + i], refs[4 + i], sem.at[1, i]) for i in range(4)]
    for copy in arrive:
        copy.start()
    for i in range(4):
        arrive[i].wait()
        leave[i].start()
    for copy in leave:
        copy.wait()


def per_device(n, *args):
    queries, text_keys, latent = args[0], args[7], args[11]
    args = (*args[:12], jnp.swapaxes(args[12], 1, 2))
    rows, features = queries.shape[2:]
    heads = features // HEAD
    local = heads // n
    text, width = text_keys.shape[2:]
    channels = latent.shape[2]
    tokens = 2 * n * rows

    def kernel(*refs):
        body(n, rows, heads, *refs)

    anywhere = pl.BlockSpec(memory_space=pl.ANY)
    raw = pltpu.VMEM((2, rows, features), BF16)
    gain = pltpu.VMEM((1, features), F32)
    source = pltpu.VMEM((2, heads, rows, HEAD), BF16)
    landed = pltpu.VMEM((local, n, 2, rows, HEAD), BF16)
    merged = pltpu.VMEM((local, tokens, HEAD), BF16)
    dma = pltpu.SemaphoreType.DMA
    results = pl.pallas_call(
        kernel,
        out_shape=(
            jax.ShapeDtypeStruct(latent.shape, F32),
            jax.ShapeDtypeStruct(latent.shape, BF16),
            jax.ShapeDtypeStruct(text_keys.shape, BF16),
            jax.ShapeDtypeStruct(text_keys.shape, BF16),
        ),
        in_specs=[anywhere] * len(args),
        out_specs=(anywhere,) * 4,
        scratch_shapes=[
            raw, raw, raw, gain, gain, gain,
            pltpu.VMEM((text, width), BF16), pltpu.VMEM((text, width), BF16),
            pltpu.SMEM((1, 1, 1), jnp.int32), pltpu.SMEM((1, 1), jnp.int32),
            pltpu.VMEM((rows, channels), F32), pltpu.VMEM((channels, width), BF16),
            source, source, source,
            pltpu.VMEM((n, 2, rows, width), BF16), landed, landed, landed,
            merged, merged, merged, merged,
            pltpu.VMEM((local, tokens, HEAD), F32), pltpu.VMEM((4 * rows, width), BF16),
            pltpu.VMEM((rows, HEAD), F32), pltpu.VMEM((rows, HEAD), F32),
            pltpu.VMEM((text, width), BF16), pltpu.VMEM((text, width), BF16),
            pltpu.VMEM((2 * HEAD, width), BF16), pltpu.VMEM((1, HEAD), F32), pltpu.VMEM((n, 1, HEAD), F32),
            pltpu.VMEM((n, 2, rows, HEAD), BF16), pltpu.VMEM((2, n, rows, HEAD), BF16),
            pltpu.VMEM((3, HEAD, HEAD), BF16), pltpu.VMEM((2, rows, channels), F32),
            pltpu.VMEM((rows, channels), F32), pltpu.VMEM((rows, channels), BF16),
            dma((12,)), dma((5, n, 2)), dma((5, n, 2)), dma((n,)), dma((n,)), dma((3,)), dma((3,)), dma,
        ],
        compiler_params=pltpu.CompilerParams(
            collective_id=0, has_side_effects=True, vmem_limit_bytes=60 * 1024 * 1024
        ),
        cost_estimate=pl.CostEstimate(
            flops=1_000_000_000, bytes_accessed=4_000_000, transcendentals=2_000_000
        ),
    )(*args)
    return pl.pallas_call(
        hand_on,
        out_shape=tuple(jax.ShapeDtypeStruct(r.shape, r.dtype) for r in results),
        in_specs=[anywhere] * 4,
        out_specs=(anywhere,) * 4,
        scratch_shapes=[*(pltpu.VMEM(r.shape, r.dtype) for r in results), dma((2, 4))],
        compiler_params=pltpu.CompilerParams(vmem_limit_bytes=60 * 1024 * 1024),
    )(*results)


def solution(mesh):
    token_spec = P("expert", None, ("rep", "cfg", "sp"), None)
    text_spec = P("expert", "cfg", "rep", "sp")
    latent_spec = P("expert", ("rep", "cfg", "sp"), None)
    gain_spec = P("expert", None)
    in_specs = (
        *(token_spec,) * 4,
        *(gain_spec,) * 3,
        text_spec,
        text_spec,
        P("expert", "cfg", "rep"),
        P("expert", "rep"),
        latent_spec,
        P("expert", "sp", None),
    )
    out_specs = (latent_spec, latent_spec, text_spec, text_spec)
    count = mesh.shape["sp"]

    def run(*args):
        return per_device(count, *args)

    return jax.shard_map(run, mesh=mesh, in_specs=in_specs, out_specs=out_specs, check_vma=False)
```
